32 devices in a mesh: groups: 2 (over y), row: 8 (over z, x), col: 2 (over core).
Axes of the slice: x: 2, y: 2, z: 4, core: 2. Of those that a mesh axis runs over, the one named last changes fastest.
Arguments:
- hidden: bfloat16 [128, 14336], P(('groups', 'row'), 'col'), parts along dimension 0, may hold values from -6 to 6
- cotangent: bfloat16 [128, 8192], P(('groups', 'row')), parts along dimension 0, may hold values from -6 to 6
- weight_t: bfloat16 [8192, 14336], P('row', 'col'), may hold values from -0.0625 to 0.0625
- block_mask: int32 [32, 56], replicated, may hold values 0 or 1
Outputs:
- output: bfloat16 [128, 8192], P(('groups', 'col'), 'row'), parts along dimension 0
- weight_grad: float32 [16384, 14336], P(('groups', 'row'), 'col'), parts along dimension 0
The draws below stay inside these ranges and needn't reach their ends.
There are 2 independent parts, one for each index of `groups`. The reference program is written for one: setup_inputs(seed, part) draws one part's arguments, and reference() takes and returns one part's arrays. A program takes and returns all parts, laid end to end along the dimension named above; an argument that names none is the same for every part. Nothing has to cross between parts.
All inputs are finite; a program needn't handle non-finite values.
Results may differ from the reference program's by a relative error of at most 0.001.
Values may be sent and summed in bfloat16 or wider, within the bound.
A program may use at most 128 MiB of HBM per device.

```python
import jax
import jax.numpy as jnp

D = 8192
FF = 14336
BLOCK = 256
TOKENS = 64


def place_ends(values, own_key, low, top_value):
    longest = values.shape.index(max(values.shape))
    spots = []
    for shift in (0, 1):
        where = [jax.random.randint(jax.random.fold_in(own_key, axis), (), 0, length) for axis, length in enumerate(values.shape)]
        where[longest] = (where[longest] + shift) % values.shape[longest]
        spots.append(tuple(where))
    return values.at[spots[0]].set(low).at[spots[1]].set(top_value)


def with_spikes(result, key, source, target, blocks, factor):
    def block_of(dim):
        return (jnp.arange(result.shape[dim]) // (result.shape[dim] // blocks)).reshape((-1,) + (1,) * (result.ndim - 1 - dim))

    one_side = jax.random.permutation(key, blocks)[block_of(target)]
    second = (block_of(target) + blocks // 2) % blocks
    return jnp.where((block_of(source) == one_side) | (block_of(source) == second), factor * result, result)


def steps_of(own_key, shape, cuts, smallest, top_value):
    factor_of = 1.0
    for dim, shards_of in cuts:
        heights = jax.random.uniform(jax.random.fold_in(jax.random.fold_in(own_key, 6), dim), (shards_of,), jnp.float32, smallest / len(cuts), top_value / len(cuts))
        factor_of = factor_of * jnp.repeat(jnp.exp(heights), shape[dim] // shards_of).reshape((-1,) + (1,) * (len(shape) - 1 - dim))
    return factor_of


def centred(own_key, extent, spread, bound, cuts=(), held_as=jnp.bfloat16):
    level = steps_of(own_key, extent, cuts, -0.22, 0.18) if cuts else 1.0
    entries = jax.random.normal(own_key, extent, jnp.float32) * spread * level
    return jnp.minimum(jnp.maximum(entries, -bound), bound).astype(held_as)


def gaussian_with(key, shape, deviation, bound, shards, heavy, kind=jnp.bfloat16):
    drawn = deviation * jax.random.normal(key, shape, jnp.float32)
    if shards:
        drawn = drawn * steps_of(key, shape, shards, -0.22, 0.18)
    return jnp.clip(with_spikes(drawn, jax.random.fold_in(key, 3), *heavy), -bound, bound).astype(kind)


def setup_inputs(seed: int = 0, part: int = 0) -> dict:
    seeds = jax.random.split(jax.random.key(seed), 5)
    part_splits = jax.random.split(jax.random.fold_in(seeds[4], part), 5)
    hidden = centred(part_splits[0], (TOKENS, FF), 1.0, 6.0, ((0, 8), (1, 2)))
    cotangent = gaussian_with(part_splits[1], (TOKENS, D), 1.0, 6.0, ((0, 8),), (0, 1, 8, 2.0))
    weight_t = centred(seeds[2], (D, FF), (FF // 2) ** -0.5, 0.0625, ((0, 8), (1, 2)))
    block_mask = place_ends((jax.random.randint(seeds[3], (D // BLOCK, FF // BLOCK), 0, 2) < 1).astype(jnp.int32), jax.random.fold_in(seeds[3], 1), 0, 1)
    return dict(hidden=hidden, cotangent=cotangent, weight_t=weight_t, block_mask=block_mask)


def expand_mask(block_mask):
    tiles = jnp.ones((BLOCK, BLOCK), jnp.bfloat16)
    return jnp.kron(block_mask.astype(jnp.bfloat16), tiles)


def reference(hidden, cotangent, weight_t, block_mask):
    keep = expand_mask(block_mask)
    kept = weight_t * keep
    output = jax.lax.dot_general(hidden, kept, (((1,), (1,)), ((), ())), preferred_element_type=jnp.float32).astype(jnp.bfloat16)
    grads = jax.lax.dot_general(cotangent, hidden, (((0,), (0,)), ((), ())), preferred_element_type=jnp.float32)
    weight_grad = grads * keep.astype(jnp.float32)
    return output, weight_grad
```

```python
import functools

import jax
import jax.numpy as jnp
from jax import lax
from jax.experimental import pallas as pl
from jax.experimental.pallas import tpu as pltpu
from jax.sharding import PartitionSpec as P

BLOCK = 256
CHUNK = 1024


def tile_keep(block_mask, row_start, rows, col_start, cols):
    row_ids = (row_start + jnp.arange(rows, dtype=jnp.int32)) // BLOCK
    col_ids = (col_start + jnp.arange(cols, dtype=jnp.int32)) // BLOCK
    row_pick = (
        row_ids[:, None] == jnp.arange(block_mask.shape[0], dtype=jnp.int32)[None, :]
    ).astype(jnp.bfloat16)
    col_pick = (
        jnp.arange(block_mask.shape[1], dtype=jnp.int32)[:, None] == col_ids[None, :]
    ).astype(jnp.bfloat16)
    narrow = jnp.dot(
        row_pick, block_mask.astype(jnp.bfloat16), preferred_element_type=jnp.float32
    ).astype(jnp.bfloat16)
    return jnp.dot(narrow, col_pick, preferred_element_type=jnp.float32).astype(jnp.bfloat16)


def general(hidden, cotangent, weight_t, block_mask):
    feat_rows, hid_cols = weight_t.shape
    row_index = lax.axis_index("row")
    col_index = lax.axis_index("col")
    keep = tile_keep(block_mask, row_index * feat_rows, feat_rows, col_index * hid_cols, hid_cols)
    kept = weight_t * keep
    cot_feat = lax.all_to_all(cotangent.T, "row", split_axis=0, concat_axis=1, tiled=True)
    piece = lax.all_gather(hidden, "row", axis=0, tiled=True)
    part = lax.dot_general(
        piece, kept, (((1,), (1,)), ((), ())), preferred_element_type=jnp.float32
    )
    grad = jnp.dot(cot_feat, piece, preferred_element_type=jnp.float32)
    output = lax.psum_scatter(part, "col", scatter_dimension=0, tiled=True).astype(jnp.bfloat16)
    return output, grad * keep.astype(jnp.float32)


def exchange(
    n,
    hidden_ref, cot_ref, weight_ref, mask_ref,
    gathered, cot_feat, out_ref,
    weight, total, other_part,
    weight_sem, hid_send, hid_recv, cot_send, cot_recv, pair_send, pair_recv,
):
    rows, cols = hidden_ref.shape
    feats = weight_ref.shape[0]
    f_tiles = feats // BLOCK
    chunks = cols // CHUNK
    tiles = CHUNK // BLOCK
    half_feats = feats // 2
    tokens = n * rows
    me = lax.axis_index("row")
    core = lax.axis_index("col")
    half = n // 2

    side = lax.rem(me, 2)
    spot = jnp.where(side == 0, me // 2, n - 1 - me // 2)

    def row_of(place):
        place = lax.rem(place + 2 * n, n)
        return jnp.where(place < half, 2 * place, 2 * (n - 1 - place) + 1)

    heads = [row_of(spot + 1), row_of(spot - 1)]

    def span(c):
        return pl.ds(c * CHUNK, CHUNK)

    loads = []
    for c in range(chunks):
        load = pltpu.make_async_copy(
            weight_ref.at[:, span(c)], weight.at[:, span(c)], weight_sem.at[c]
        )
        load.start()
        loads.append(load)

    barrier = pltpu.get_barrier_semaphore()
    for d in range(1, n):
        pl.semaphore_signal(
            barrier, inc=1, device_id={"row": lax.rem(me + d, n)},
            device_id_type=pl.DeviceIdType.MESH,
        )
    pl.semaphore_signal(
        barrier, inc=1, device_id={"col": 1 - core}, device_id_type=pl.DeviceIdType.MESH
    )
    pl.semaphore_wait(barrier, n)

    def hop(way, h, c):
        source = row_of(spot - (h - 1)) if way == 0 else row_of(spot + (h - 1))
        here = gathered.at[source, :, span(c)]
        return pltpu.make_async_remote_copy(
            src_ref=hidden_ref.at[:, span(c)] if h == 1 else here,
            dst_ref=here,
            send_sem=hid_send.at[way, h - 1, c],
            recv_sem=hid_recv.at[way, h - 1, c],
            device_id={"row": heads[way]},
            device_id_type=pl.DeviceIdType.MESH,
        )

    def arrival(way, h, c):
        source = row_of(spot - h) if way == 0 else row_of(spot + h)
        here = gathered.at[source, :, span(c)]
        return pltpu.make_async_remote_copy(
            src_ref=here,
            dst_ref=here,
            send_sem=hid_send.at[way, h - 1, c],
            recv_sem=hid_recv.at[way, h - 1, c],
            device_id={"row": heads[way]},
            device_id_type=pl.DeviceIdType.MESH,
        )

    sent = []

    def send(way, h, c):
        copy = hop(way, h, c)
        copy.start()
        sent.append(copy)

    ahead = min(2, chunks)
    for c in range(ahead):
        for way in range(2):
            send(way, 1, c)

    my_half = pl.ds(pl.multiple_of(core * half_feats, 128), half_feats)
    cot_copies = []
    for d in range(1, n):
        to = lax.rem(me + d, n)
        piece = pl.ds(pl.multiple_of(to * feats + core * half_feats, 128), half_feats)
        copy = pltpu.make_async_remote_copy(
            src_ref=cot_ref.at[:, piece],
            dst_ref=cot_feat.at[me, :, my_half],
            send_sem=cot_send.at[d - 1],
            recv_sem=cot_recv.at[d - 1],
            device_id={"row": to},
            device_id_type=pl.DeviceIdType.MESH,
        )
        copy.start()
        cot_copies.append(copy)
    own = pl.ds(pl.multiple_of(me * feats + core * half_feats, 128), half_feats)
    cot_feat[me, :, my_half] = cot_ref[:, own]
    gathered[me, :, :] = hidden_ref[...]
    total[...] = jnp.zeros_like(total)

    def multiply(c):
        loads[c].wait()
        block = gathered[:, :, c * CHUNK:(c + 1) * CHUNK].reshape(tokens, CHUNK)
        for f in range(f_tiles):
            parts = []
            for t in range(tiles):
                factor = mask_ref[me * f_tiles + f, core * (chunks * tiles) + c * tiles + t]
                factor = factor.astype(jnp.float32).astype(jnp.bfloat16)
                parts.append(block[:, t * BLOCK:(t + 1) * BLOCK] * factor)
            picked = jnp.concatenate(parts, axis=1)
            lanes = slice(f * BLOCK, (f + 1) * BLOCK)
            total[:, lanes] += lax.dot_general(
                picked,
                weight[lanes, c * CHUNK:(c + 1) * CHUNK],
                (((1,), (1,)), ((), ())),
                preferred_element_type=jnp.float32,
            )

    def ways(h, c):
        return [0, 1] if h < half else [c % 2]

    for t in range(chunks + half):
        if t + ahead < chunks:
            for way in range(2):
                send(way, 1, t + ahead)
        for h in range(1, half + 1):
            c = t - (h - 1)
            if 0 <= c < chunks:
                for way in ways(h, c):
                    arrival(way, h, c).wait_recv()
                    if h < half and way in ways(h + 1, c):
                        send(way, h + 1, c)
        if t == half:
            for copy in cot_copies:
                copy.wait_recv()
            mine = cot_feat.at[:, :, my_half]
            cot_pair = pltpu.make_async_remote_copy(
                src_ref=mine, dst_ref=mine,
                send_sem=pair_send.at[0], recv_sem=pair_recv.at[0],
                device_id={"col": 1 - core}, device_id_type=pl.DeviceIdType.MESH,
            )
            cot_pair.start()
        c = t - (half - 1)
        if 0 <= c < chunks:
            multiply(c)

    kept_rows = tokens // 2
    pair = pltpu.make_async_remote_copy(
        src_ref=total.at[pl.ds(pl.multiple_of((1 - core) * kept_rows, 8), kept_rows)],
        dst_ref=other_part,
        send_sem=pair_send.at[1], recv_sem=pair_recv.at[1],
        device_id={"col": 1 - core}, device_id_type=pl.DeviceIdType.MESH,
    )
    pair.start()
    for copy in sent:
        copy.wait_send()
    for copy in cot_copies:
        copy.wait_send()
    cot_pair.wait()
    pair.wait()
    mine = total[pl.ds(pl.multiple_of(core * kept_rows, 8), kept_rows), :]
    out_ref[...] = (mine + other_part[...]).astype(out_ref.dtype)


def outer(splits, gathered, cot_feat, mask_ref, grad_ref):
    n, rows, cols = gathered.shape
    tokens = n * rows
    feats = cot_feat.shape[2]
    f_tiles = feats // BLOCK
    me = lax.axis_index("row")
    core = lax.axis_index("col")
    f = pl.program_id(0)
    part = pl.program_id(1)
    width = cols // splits
    tiles = width // BLOCK
    left = cot_feat[:, :, pl.ds(pl.multiple_of(f * BLOCK, BLOCK), BLOCK)].reshape(tokens, BLOCK)
    for t in range(tiles):
        k = part * tiles + t
        factor = mask_ref[me * f_tiles + f, core * (tiles * splits) + k]
        factor = factor.astype(jnp.float32).astype(jnp.bfloat16)
        block = gathered[:, :, pl.ds(pl.multiple_of(k * BLOCK, BLOCK), BLOCK)]
        grad_ref[:, t * BLOCK:(t + 1) * BLOCK] = lax.dot_general(
            left,
            block.reshape(tokens, BLOCK) * factor,
            (((0,), (0,)), ((), ())),
            preferred_element_type=jnp.float32,
        )


def tiled(n, hidden, cotangent, weight_t, block_mask):
    rows, cols = hidden.shape
    feats = weight_t.shape[0]
    tokens = n * rows
    half = n // 2
    chunks = cols // CHUNK
    vmem = pl.BlockSpec(memory_space=pltpu.VMEM)
    smem = pl.BlockSpec(memory_space=pltpu.SMEM)
    gathered, cot_feat, output = pl.pallas_call(
        functools.partial(exchange, n),
        out_shape=(
            jax.ShapeDtypeStruct((n, rows, cols), jnp.bfloat16),
            jax.ShapeDtypeStruct((n, rows, feats), jnp.bfloat16),
            jax.ShapeDtypeStruct((tokens // 2, feats), jnp.bfloat16),
        ),
        in_specs=[vmem, vmem, pl.BlockSpec(memory_space=pl.ANY), smem],
        out_specs=(vmem, vmem, vmem),
        scratch_shapes=[
            pltpu.VMEM((feats, cols), jnp.bfloat16),
            pltpu.VMEM((tokens, feats), jnp.float32),
            pltpu.VMEM((tokens // 2, feats), jnp.float32),
            pltpu.SemaphoreType.DMA((chunks,)),
            pltpu.SemaphoreType.DMA((2, half, chunks)),
            pltpu.SemaphoreType.DMA((2, half, chunks)),
            pltpu.SemaphoreType.DMA((n - 1,)),
            pltpu.SemaphoreType.DMA((n - 1,)),
            pltpu.SemaphoreType.DMA((2,)),
            pltpu.SemaphoreType.DMA((2,)),
        ],
        compiler_params=pltpu.CompilerParams(
            collective_id=0, has_side_effects=True, vmem_limit_bytes=40 * 1024 * 1024
        ),
        cost_estimate=pl.CostEstimate(
            flops=2 * tokens * feats * cols,
            bytes_accessed=2 * feats * cols,
            transcendentals=0,
        ),
    )(hidden, cotangent, weight_t, block_mask)
    splits = 4
    grad = pl.pallas_call(
        functools.partial(outer, splits),
        grid=(feats // BLOCK, splits),
        out_shape=jax.ShapeDtypeStruct((feats, cols), jnp.float32),
        in_specs=[vmem, vmem, smem],
        out_specs=pl.BlockSpec((BLOCK, cols // splits), lambda f, s: (f, s)),
        compiler_params=pltpu.CompilerParams(vmem_limit_bytes=40 * 1024 * 1024),
        cost_estimate=pl.CostEstimate(
            flops=2 * tokens * feats * cols,
            bytes_accessed=4 * feats * cols,
            transcendentals=0,
        ),
    )(gathered, cot_feat, block_mask)
    return output, grad


def solution(mesh):
    n = mesh.shape["row"]

    def local(hidden, cotangent, weight_t, block_mask):
        feats, cols = weight_t.shape
        whole_tiles = feats % BLOCK == 0 and cols % CHUNK == 0
        if whole_tiles and n % 2 == 0 and mesh.shape["col"] == 2:
            return tiled(n, hidden, cotangent, weight_t, block_mask)
        return general(hidden, cotangent, weight_t, block_mask)

    return jax.shard_map(
        local,
        mesh=mesh,
        in_specs=(P(("groups", "row"), "col"), P(("groups", "row"), None), P("row", "col"), P()),
        out_specs=(P(("groups", "col"), "row"), P(("groups", "row"), "col")),
        check_vma=False,
    )
```

```python
import functools

import jax
import jax.numpy as jnp
from jax import lax
from jax.experimental import pallas as pl
from jax.experimental.pallas import tpu as pltpu
from jax.sharding import PartitionSpec as P

BLOCK = 256
CHUNKS = 4
HEIGHT = 128


def tile_keep(block_mask, row_start, rows, col_start, cols):
    row_ids = (row_start + jnp.arange(rows, dtype=jnp.int32)) // BLOCK
    col_ids = (col_start + jnp.arange(cols, dtype=jnp.int32)) // BLOCK
    row_pick = (
        row_ids[:, None] == jnp.arange(block_mask.shape[0], dtype=jnp.int32)[None, :]
    ).astype(jnp.bfloat16)
    col_pick = (
        jnp.arange(block_mask.shape[1], dtype=jnp.int32)[:, None] == col_ids[None, :]
    ).astype(jnp.bfloat16)
    narrow = jnp.dot(
        row_pick, block_mask.astype(jnp.bfloat16), preferred_element_type=jnp.float32
    ).astype(jnp.bfloat16)
    return jnp.dot(narrow, col_pick, preferred_element_type=jnp.float32).astype(jnp.bfloat16)


def general(hidden, cotangent, weight_t, block_mask):
    feat_rows, hid_cols = weight_t.shape
    row_index = lax.axis_index("row")
    col_index = lax.axis_index("col")
    keep = tile_keep(block_mask, row_index * feat_rows, feat_rows, col_index * hid_cols, hid_cols)
    kept = weight_t * keep
    cot_feat = lax.all_to_all(cotangent.T, "row", split_axis=0, concat_axis=1, tiled=True)
    piece = lax.all_gather(hidden, "row", axis=0, tiled=True)
    part = lax.dot_general(
        piece, kept, (((1,), (1,)), ((), ())), preferred_element_type=jnp.float32
    )
    grad = jnp.dot(cot_feat, piece, preferred_element_type=jnp.float32)
    output = lax.psum_scatter(part, "col", scatter_dimension=0, tiled=True).astype(jnp.bfloat16)
    return output, grad * keep.astype(jnp.float32)


def exchange(
    n,
    hidden_ref, cot_ref, weight_ref, mask_ref,
    gathered, cot_feat, mask_out, out_ref,
    weight, total, other_part, mask,
    weight_sem, hid_send, hid_recv, cot_send, cot_recv, pair_send, pair_recv, own_sem,
):
    rows, cols = hidden_ref.shape
    feats = weight_ref.shape[0]
    f_tiles = feats // BLOCK
    chunk = cols // CHUNKS
    tiles = chunk // BLOCK
    half_feats = feats // 2
    tokens = n * rows
    me = lax.axis_index("row")
    core = lax.axis_index("col")
    half = n // 2
    mesh_id = pl.DeviceIdType.MESH

    spot = jnp.where(lax.rem(me, 2) == 0, me // 2, n - 1 - me // 2)

    def row_of(place):
        place = lax.rem(place + n, n)
        return jnp.where(place < half, 2 * place, 2 * (n - 1 - place) + 1)

    places = [
        [row_of(spot - back) for back in range(half + 1)],
        [row_of(spot + back) for back in range(half + 1)],
    ]
    heads = [places[1][1], places[0][1]]

    barrier = pltpu.get_barrier_semaphore()
    for d in range(1, n):
        pl.semaphore_signal(
            barrier, inc=1, device_id={"row": lax.rem(me + d, n)}, device_id_type=mesh_id
        )
    pl.semaphore_signal(barrier, inc=1, device_id={"col": 1 - core}, device_id_type=mesh_id)

    def span(c):
        return pl.ds(c * chunk, chunk)

    my_half = pl.ds(pl.multiple_of(core * half_feats, 128), half_feats)

    def cot_piece(to):
        return cot_ref.at[:, pl.ds(pl.multiple_of(to * feats + core * half_feats, 128), half_feats)]

    pl.semaphore_wait(barrier, n)

    def hop(way, h, c, back):
        here = gathered.at[places[way][back], :, span(c)]
        return pltpu.make_async_remote_copy(
            src_ref=hidden_ref.at[:, span(c)] if back == 0 else here,
            dst_ref=here,
            send_sem=hid_send.at[way],
            recv_sem=hid_recv.at[way, h - 1, c],
            device_id={"row": heads[way]},
            device_id_type=mesh_id,
        )

    for c in range(CHUNKS):
        for way in range(2):
            hop(way, 1, c, 0).start()

    cot_copies = []
    for d in range(1, n):
        to = lax.rem(me + d, n)
        copy = pltpu.make_async_remote_copy(
            src_ref=cot_piece(to),
            dst_ref=cot_feat.at[me, :, my_half],
            send_sem=cot_send.at[d - 1],
            recv_sem=cot_recv.at[d - 1],
            device_id={"row": to},
            device_id_type=mesh_id,
        )
        copy.start()
        cot_copies.append(copy)
    locals_ = [
        pltpu.make_async_copy(hidden_ref, gathered.at[me], own_sem.at[0]),
        pltpu.make_async_copy(cot_piece(me), cot_feat.at[me, :, my_half], own_sem.at[1]),
        pltpu.make_async_copy(mask_ref, mask, own_sem.at[2]),
        pltpu.make_async_copy(mask_ref, mask_out, own_sem.at[3]),
    ]
    for copy in locals_:
        copy.start()
    loads = []
    for c in range(CHUNKS):
        load = pltpu.make_async_copy(
            weight_ref.at[:, span(c)], weight.at[:, span(c)], weight_sem.at[c]
        )
        load.start()
        loads.append(load)
    total[...] = jnp.zeros_like(total)

    def last_way(c):
        return 0 if c < CHUNKS // 2 else 1

    for h in range(1, half):
        for c in range(CHUNKS):
            for way in range(2):
                hop(way, h, c, h).wait_recv()
                if h + 1 < half or last_way(c) == way:
                    hop(way, h + 1, c, h).start()
    for copy in locals_:
        copy.wait()
    for copy in cot_copies:
        copy.wait_recv()
    mine = cot_feat.at[:, :, my_half]
    cot_pair = pltpu.make_async_remote_copy(
        src_ref=mine, dst_ref=mine,
        send_sem=pair_send.at[0], recv_sem=pair_recv.at[0],
        device_id={"col": 1 - core}, device_id_type=mesh_id,
    )
    cot_pair.start()

    def multiply(c):
        loads[c].wait()
        block = gathered[:, :, c * chunk:(c + 1) * chunk].reshape(tokens, chunk)
        for f in range(f_tiles):
            parts = []
            for t in range(tiles):
                factor = mask[me * f_tiles + f, core * (CHUNKS * tiles) + c * tiles + t]
                factor = factor.astype(jnp.float32).astype(jnp.bfloat16)
                parts.append(block[:, t * BLOCK:(t + 1) * BLOCK] * factor)
            picked = jnp.concatenate(parts, axis=1)
            lanes = slice(f * BLOCK, (f + 1) * BLOCK)
            total[:, lanes] += lax.dot_general(
                picked,
                weight[lanes, c * chunk:(c + 1) * chunk],
                (((1,), (1,)), ((), ())),
                preferred_element_type=jnp.float32,
            )

    for i in range(CHUNKS // 2):
        for c in (i, i + CHUNKS // 2):
            hop(last_way(c), half, c, half).wait_recv()
            multiply(c)

    kept_rows = tokens // 2
    pair = pltpu.make_async_remote_copy(
        src_ref=total.at[pl.ds(pl.multiple_of((1 - core) * kept_rows, 8), kept_rows)],
        dst_ref=other_part,
        send_sem=pair_send.at[1], recv_sem=pair_recv.at[1],
        device_id={"col": 1 - core}, device_id_type=mesh_id,
    )
    pair.start()
    for way in range(2):
        all_sent = gathered.at[pl.ds(0, n - 1), :, pl.ds(0, cols // 2)]
        pltpu.make_async_remote_copy(
            src_ref=all_sent, dst_ref=all_sent,
            send_sem=hid_send.at[way], recv_sem=hid_recv.at[way, 0, 0],
            device_id={"row": heads[way]}, device_id_type=mesh_id,
        ).wait_send()
    for copy in cot_copies:
        copy.wait_send()
    cot_pair.wait()
    pair.wait()
    mine = total[pl.ds(pl.multiple_of(core * kept_rows, 8), kept_rows), :]
    out_ref[...] = (mine + other_part[...]).astype(out_ref.dtype)


def outer(gathered, cot_feat, mask_ref, grad_ref):
    n, rows, cols = gathered.shape
    tokens = n * rows
    feats = cot_feat.shape[2]
    f_tiles = feats // BLOCK
    height = grad_ref.shape[0]
    tiles = cols // BLOCK
    me = lax.axis_index("row")
    core = lax.axis_index("col")
    step = pl.program_id(0)
    f = step // (BLOCK // height)
    left = cot_feat[:, :, pl.ds(pl.multiple_of(step * height, height), height)]
    left = left.reshape(tokens, height)
    for t in range(tiles):
        factor = mask_ref[me * f_tiles + f, core * tiles + t]
        factor = factor.astype(jnp.float32).astype(jnp.bfloat16)
        lanes = slice(t * BLOCK, (t + 1) * BLOCK)
        grad_ref[:, lanes] = lax.dot_general(
            left,
            gathered[:, :, lanes].reshape(tokens, BLOCK) * factor,
            (((0,), (0,)), ((), ())),
            preferred_element_type=jnp.float32,
        )


def grad_of(gathered, cot_feat, block_mask):
    n, rows, cols = gathered.shape
    feats = cot_feat.shape[2]
    vmem = pl.BlockSpec(memory_space=pltpu.VMEM)
    return pl.pallas_call(
        outer,
        grid=(feats // HEIGHT,),
        out_shape=jax.ShapeDtypeStruct((feats, cols), jnp.float32),
        in_specs=[vmem, vmem, pl.BlockSpec(memory_space=pltpu.SMEM)],
        out_specs=pl.BlockSpec((HEIGHT, cols), lambda step: (step, 0)),
        compiler_params=pltpu.CompilerParams(vmem_limit_bytes=40 * 1024 * 1024),
        cost_estimate=pl.CostEstimate(
            flops=2 * n * rows * feats * cols,
            bytes_accessed=4 * feats * cols,
            transcendentals=0,
        ),
    )(gathered, cot_feat, block_mask)


def tiled(n, hidden, cotangent, weight_t, block_mask):
    rows, cols = hidden.shape
    feats = weight_t.shape[0]
    tokens = n * rows
    half = n // 2
    vmem = pl.BlockSpec(memory_space=pltpu.VMEM)
    hbm = pl.BlockSpec(memory_space=pltpu.HBM)
    gathered, cot_feat, mask, output = pl.pallas_call(
        functools.partial(exchange, n),
        out_shape=(
            jax.ShapeDtypeStruct((n, rows, cols), jnp.bfloat16),
            jax.ShapeDtypeStruct((n, rows, feats), jnp.bfloat16),
            jax.ShapeDtypeStruct(block_mask.shape, jnp.int32),
            jax.ShapeDtypeStruct((tokens // 2, feats), jnp.bfloat16),
        ),
        in_specs=[hbm, hbm, hbm, hbm],
        out_specs=(vmem, vmem, vmem, vmem),
        scratch_shapes=[
            pltpu.VMEM((feats, cols), jnp.bfloat16),
            pltpu.VMEM((tokens, feats), jnp.float32),
            pltpu.VMEM((tokens // 2, feats), jnp.float32),
            pltpu.SMEM(block_mask.shape, jnp.int32),
            pltpu.SemaphoreType.DMA((CHUNKS,)),
            pltpu.SemaphoreType.DMA((2,)),
            pltpu.SemaphoreType.DMA((2, half, CHUNKS)),
            pltpu.SemaphoreType.DMA((n - 1,)),
            pltpu.SemaphoreType.DMA((n - 1,)),
            pltpu.SemaphoreType.DMA((2,)),
            pltpu.SemaphoreType.DMA((2,)),
            pltpu.SemaphoreType.DMA((4,)),
        ],
        compiler_params=pltpu.CompilerParams(
            collective_id=0, has_side_effects=True, vmem_limit_bytes=40 * 1024 * 1024
        ),
        cost_estimate=pl.CostEstimate(
            flops=2 * tokens * feats * cols,
            bytes_accessed=2 * feats * cols,
            transcendentals=0,
        ),
    )(hidden, cotangent, weight_t, block_mask)
    return output, grad_of(gathered, cot_feat, mask)


def solution(mesh):
    n = mesh.shape["row"]

    def local(hidden, cotangent, weight_t, block_mask):
        feats, cols = weight_t.shape
        whole_tiles = feats % BLOCK == 0 and cols % (CHUNKS * BLOCK) == 0
        if whole_tiles and n % 2 == 0 and mesh.shape["col"] == 2:
            return tiled(n, hidden, cotangent, weight_t, block_mask)
        return general(hidden, cotangent, weight_t, block_mask)

    return jax.shard_map(
        local,
        mesh=mesh,
        in_specs=(P(("groups", "row"), "col"), P(("groups", "row"), None), P("row", "col"), P()),
        out_specs=(P(("groups", "col"), "row"), P(("groups", "row"), "col")),
        check_vma=False,
    )
```

```python
import functools

import jax
import jax.numpy as jnp
from jax import lax
from jax.experimental import pallas as pl
from jax.experimental.pallas import tpu as pltpu
from jax.sharding import PartitionSpec as P

BLOCK = 256
CHUNKS = 4
HEIGHT = 128


def tile_keep(block_mask, row_start, rows, col_start, cols):
    row_ids = (row_start + jnp.arange(rows, dtype=jnp.int32)) // BLOCK
    col_ids = (col_start + jnp.arange(cols, dtype=jnp.int32)) // BLOCK
    row_pick = (
        row_ids[:, None] == jnp.arange(block_mask.shape[0], dtype=jnp.int32)[None, :]
    ).astype(jnp.bfloat16)
    col_pick = (
        jnp.arange(block_mask.shape[1], dtype=jnp.int32)[:, None] == col_ids[None, :]
    ).astype(jnp.bfloat16)
    narrow = jnp.dot(
        row_pick, block_mask.astype(jnp.bfloat16), preferred_element_type=jnp.float32
    ).astype(jnp.bfloat16)
    return jnp.dot(narrow, col_pick, preferred_element_type=jnp.float32).astype(jnp.bfloat16)


def general(hidden, cotangent, weight_t, block_mask):
    feat_rows, hid_cols = weight_t.shape
    row_index = lax.axis_index("row")
    col_index = lax.axis_index("col")
    keep = tile_keep(block_mask, row_index * feat_rows, feat_rows, col_index * hid_cols, hid_cols)
    kept = weight_t * keep
    cot_feat = lax.all_to_all(cotangent.T, "row", split_axis=0, concat_axis=1, tiled=True)
    piece = lax.all_gather(hidden, "row", axis=0, tiled=True)
    part = lax.dot_general(
        piece, kept, (((1,), (1,)), ((), ())), preferred_element_type=jnp.float32
    )
    grad = jnp.dot(cot_feat, piece, preferred_element_type=jnp.float32)
    output = lax.psum_scatter(part, "col", scatter_dimension=0, tiled=True).astype(jnp.bfloat16)
    return output, grad * keep.astype(jnp.float32)


def exchange(
    n,
    hidden_ref, cot_ref, weight_ref, mask_ref,
    gathered, cot_feat, mask_out, out_ref,
    weight, total, other_part, mask,
    weight_sem, hid_send, hid_recv, cot_send, cot_recv, pair_send, pair_recv, own_sem,
):
    rows, cols = hidden_ref.shape
    feats = weight_ref.shape[0]
    f_tiles = feats // BLOCK
    chunk = cols // CHUNKS
    tiles = chunk // BLOCK
    half_feats = feats // 2
    tokens = n * rows
    me = lax.axis_index("row")
    core = lax.axis_index("col")
    half = n // 2
    mesh_id = pl.DeviceIdType.MESH

    spot = jnp.where(lax.rem(me, 2) == 0, me // 2, n - 1 - me // 2)

    def row_of(place):
        place = lax.rem(place + n, n)
        return jnp.where(place < half, 2 * place, 2 * (n - 1 - place) + 1)

    places = [
        [row_of(spot - back) for back in range(half + 1)],
        [row_of(spot + back) for back in range(half + 1)],
    ]
    heads = [places[1][1], places[0][1]]

    barrier = pltpu.get_barrier_semaphore()
    for d in range(1, n):
        pl.semaphore_signal(
            barrier, inc=1, device_id={"row": lax.rem(me + d, n)}, device_id_type=mesh_id
        )
    pl.semaphore_signal(barrier, inc=1, device_id={"col": 1 - core}, device_id_type=mesh_id)

    def span(c):
        return pl.ds(c * chunk, chunk)

    my_half = pl.ds(pl.multiple_of(core * half_feats, 128), half_feats)

    def cot_piece(to):
        return cot_ref.at[:, pl.ds(pl.multiple_of(to * feats + core * half_feats, 128), half_feats)]

    pl.semaphore_wait(barrier, n)

    def hop(way, h, c, back):
        here = gathered.at[places[way][back], :, span(c)]
        return pltpu.make_async_remote_copy(
            src_ref=hidden_ref.at[:, span(c)] if back == 0 else here,
            dst_ref=here,
            send_sem=hid_send.at[way],
            recv_sem=hid_recv.at[way, h - 1, c],
            device_id={"row": heads[way]},
            device_id_type=mesh_id,
        )

    for c in range(CHUNKS):
        for way in range(2):
            hop(way, 1, c, 0).start()

    cot_copies = []
    for d in range(1, n):
        to = lax.rem(me + d, n)
        copy = pltpu.make_async_remote_copy(
            src_ref=cot_piece(to),
            dst_ref=cot_feat.at[me, :, my_half],
            send_sem=cot_send.at[d - 1],
            recv_sem=cot_recv.at[d - 1],
            device_id={"row": to},
            device_id_type=mesh_id,
        )
        copy.start()
        cot_copies.append(copy)
    locals_ = [
        pltpu.make_async_copy(hidden_ref, gathered.at[me], own_sem.at[0]),
        pltpu.make_async_copy(cot_piece(me), cot_feat.at[me, :, my_half], own_sem.at[1]),
        pltpu.make_async_copy(mask_ref, mask, own_sem.at[2]),
        pltpu.make_async_copy(mask_ref, mask_out, own_sem.at[3]),
    ]
    for copy in locals_:
        copy.start()
    loads = []
    for c in range(CHUNKS):
        load = pltpu.make_async_copy(
            weight_ref.at[:, span(c)], weight.at[:, span(c)], weight_sem.at[c]
        )
        load.start()
        loads.append(load)
    total[...] = jnp.zeros_like(total)

    def last_way(c):
        return 0 if c < CHUNKS // 2 else 1

    for h in range(1, half):
        for c in range(CHUNKS):
            for way in range(2):
                hop(way, h, c, h).wait_recv()
                if h + 1 < half or last_way(c) == way:
                    hop(way, h + 1, c, h).start()
    for copy in locals_:
        copy.wait()
    for copy in cot_copies:
        copy.wait_recv()
    mine = cot_feat.at[:, :, my_half]
    cot_pair = pltpu.make_async_remote_copy(
        src_ref=mine, dst_ref=mine,
        send_sem=pair_send.at[0], recv_sem=pair_recv.at[0],
        device_id={"col": 1 - core}, device_id_type=mesh_id,
    )
    cot_pair.start()

    def multiply(c):
        loads[c].wait()
        block = gathered[:, :, c * chunk:(c + 1) * chunk].reshape(tokens, chunk)
        for f in range(f_tiles):
            parts = []
            for t in range(tiles):
                factor = mask[me * f_tiles + f, core * (CHUNKS * tiles) + c * tiles + t]
                factor = factor.astype(jnp.float32).astype(jnp.bfloat16)
                parts.append(block[:, t * BLOCK:(t + 1) * BLOCK] * factor)
            picked = jnp.concatenate(parts, axis=1)
            lanes = slice(f * BLOCK, (f + 1) * BLOCK)
            total[:, lanes] += lax.dot_general(
                picked,
                weight[lanes, c * chunk:(c + 1) * chunk],
                (((1,), (1,)), ((), ())),
                preferred_element_type=jnp.float32,
            )

    for i in range(CHUNKS // 2):
        for c in (i, i + CHUNKS // 2):
            hop(last_way(c), half, c, half).wait_recv()
            multiply(c)

    kept_rows = tokens // 2
    pair = pltpu.make_async_remote_copy(
        src_ref=total.at[pl.ds(pl.multiple_of((1 - core) * kept_rows, 8), kept_rows)],
        dst_ref=other_part,
        send_sem=pair_send.at[1], recv_sem=pair_recv.at[1],
        device_id={"col": 1 - core}, device_id_type=mesh_id,
    )
    pair.start()
    for way in range(2):
        all_sent = gathered.at[pl.ds(0, n - 1), :, pl.ds(0, cols // 2)]
        pltpu.make_async_remote_copy(
            src_ref=all_sent, dst_ref=all_sent,
            send_sem=hid_send.at[way], recv_sem=hid_recv.at[way, 0, 0],
            device_id={"row": heads[way]}, device_id_type=mesh_id,
        ).wait_send()
    for copy in cot_copies:
        copy.wait_send()
    cot_pair.wait()
    pair.wait()
    mine = total[pl.ds(pl.multiple_of(core * kept_rows, 8), kept_rows), :]
    out_ref[...] = (mine + other_part[...]).astype(out_ref.dtype)


def outer(gathered, cot_feat, mask_ref, grad_ref):
    n, rows, cols = gathered.shape
    tokens = n * rows
    feats = cot_feat.shape[2]
    f_tiles = feats // BLOCK
    height = grad_ref.shape[0]
    tiles = cols // BLOCK
    me = lax.axis_index("row")
    core = lax.axis_index("col")
    step = pl.program_id(0)
    f = step // (BLOCK // height)
    left = cot_feat[:, :, pl.ds(pl.multiple_of(step * height, height), height)]
    left = left.reshape(tokens, height)
    for t in range(tiles):
        factor = mask_ref[me * f_tiles + f, core * tiles + t]
        factor = factor.astype(jnp.float32).astype(jnp.bfloat16)
        lanes = slice(t * BLOCK, (t + 1) * BLOCK)
        grad_ref[:, lanes] = lax.dot_general(
            left,
            gathered[:, :, lanes].reshape(tokens, BLOCK) * factor,
            (((0,), (0,)), ((), ())),
            preferred_element_type=jnp.float32,
        )


def grad_of(gathered, cot_feat, block_mask):
    n, rows, cols = gathered.shape
    feats = cot_feat.shape[2]
    vmem = pl.BlockSpec(memory_space=pltpu.VMEM)
    return pl.pallas_call(
        outer,
        grid=(feats // HEIGHT,),
        out_shape=jax.ShapeDtypeStruct((feats, cols), jnp.float32),
        in_specs=[vmem, vmem, pl.BlockSpec(memory_space=pltpu.SMEM)],
        out_specs=pl.BlockSpec((HEIGHT, cols), lambda step: (step, 0)),
        compiler_params=pltpu.CompilerParams(vmem_limit_bytes=40 * 1024 * 1024),
        cost_estimate=pl.CostEstimate(
            flops=2 * n * rows * feats * cols,
            bytes_accessed=4 * feats * cols,
            transcendentals=0,
        ),
    )(gathered, cot_feat, block_mask)


def tiled(n, hidden, cotangent, weight_t, block_mask):
    rows, cols = hidden.shape
    feats = weight_t.shape[0]
    tokens = n * rows
    half = n // 2
    vmem = pl.BlockSpec(memory_space=pltpu.VMEM)
    hbm = pl.BlockSpec(memory_space=pltpu.HBM)
    gathered, cot_feat, mask, output = pl.pallas_call(
        functools.partial(exchange, n),
        out_shape=(
            jax.ShapeDtypeStruct((n, rows, cols), jnp.bfloat16),
            jax.ShapeDtypeStruct((n, rows, feats), jnp.bfloat16),
            jax.ShapeDtypeStruct(block_mask.shape, jnp.int32),
            jax.ShapeDtypeStruct((tokens // 2, feats), jnp.bfloat16),
        ),
        in_specs=[hbm, hbm, hbm, hbm],
        out_specs=(vmem, vmem, vmem, vmem),
        scratch_shapes=[
            pltpu.VMEM((feats, cols), jnp.bfloat16),
            pltpu.VMEM((tokens, feats), jnp.float32),
            pltpu.VMEM((tokens // 2, feats), jnp.float32),
            pltpu.SMEM(block_mask.shape, jnp.int32),
            pltpu.SemaphoreType.DMA((CHUNKS,)),
            pltpu.SemaphoreType.DMA((2,)),
            pltpu.SemaphoreType.DMA((2, half, CHUNKS)),
            pltpu.SemaphoreType.DMA((n - 1,)),
            pltpu.SemaphoreType.DMA((n - 1,)),
            pltpu.SemaphoreType.DMA((2,)),
            pltpu.SemaphoreType.DMA((2,)),
            pltpu.SemaphoreType.DMA((4,)),
        ],
        compiler_params=pltpu.CompilerParams(
            collective_id=0, has_side_effects=True, vmem_limit_bytes=40 * 1024 * 1024
        ),
        cost_estimate=pl.CostEstimate(
            flops=2 * tokens * feats * cols,
            bytes_accessed=2 * feats * cols,
            transcendentals=0,
        ),
    )(
        *(
            pltpu.with_memory_space_constraint(array, pltpu.HBM)
            for array in (hidden, cotangent, weight_t, block_mask)
        )
    )
    return output, grad_of(gathered, cot_feat, mask)


def solution(mesh):
    n = mesh.shape["row"]

    def local(hidden, cotangent, weight_t, block_mask):
        feats, cols = weight_t.shape
        whole_tiles = feats % BLOCK == 0 and cols % (CHUNKS * BLOCK) == 0
        if whole_tiles and n % 2 == 0 and mesh.shape["col"] == 2:
            return tiled(n, hidden, cotangent, weight_t, block_mask)
        return general(hidden, cotangent, weight_t, block_mask)

    return jax.shard_map(
        local,
        mesh=mesh,
        in_specs=(P(("groups", "row"), "col"), P(("groups", "row"), None), P("row", "col"), P()),
        out_specs=(P(("groups", "col"), "row"), P(("groups", "row"), "col")),
        check_vma=False,
    )
```

```python
import functools

import jax
import jax.numpy as jnp
from jax import lax
from jax.experimental import pallas as pl
from jax.experimental.pallas import tpu as pltpu
from jax.sharding import PartitionSpec as P

BLOCK = 256
CHUNKS = 14
HEIGHT = 128


def tile_keep(block_mask, row_start, rows, col_start, cols):
    row_ids = (row_start + jnp.arange(rows, dtype=jnp.int32)) // BLOCK
    col_ids = (col_start + jnp.arange(cols, dtype=jnp.int32)) // BLOCK
    row_pick = (
        row_ids[:, None] == jnp.arange(block_mask.shape[0], dtype=jnp.int32)[None, :]
    ).astype(jnp.bfloat16)
    col_pick = (
        jnp.arange(block_mask.shape[1], dtype=jnp.int32)[:, None] == col_ids[None, :]
    ).astype(jnp.bfloat16)
    narrow = jnp.dot(
        row_pick, block_mask.astype(jnp.bfloat16), preferred_element_type=jnp.float32
    ).astype(jnp.bfloat16)
    return jnp.dot(narrow, col_pick, preferred_element_type=jnp.float32).astype(jnp.bfloat16)


def general(hidden, cotangent, weight_t, block_mask):
    feat_rows, hid_cols = weight_t.shape
    row_index = lax.axis_index("row")
    col_index = lax.axis_index("col")
    keep = tile_keep(block_mask, row_index * feat_rows, feat_rows, col_index * hid_cols, hid_cols)
    kept = weight_t * keep
    cot_feat = lax.all_to_all(cotangent.T, "row", split_axis=0, concat_axis=1, tiled=True)
    piece = lax.all_gather(hidden, "row", axis=0, tiled=True)
    part = lax.dot_general(
        piece, kept, (((1,), (1,)), ((), ())), preferred_element_type=jnp.float32
    )
    grad = jnp.dot(cot_feat, piece, preferred_element_type=jnp.float32)
    output = lax.psum_scatter(part, "col", scatter_dimension=0, tiled=True).astype(jnp.bfloat16)
    return output, grad * keep.astype(jnp.float32)


def exchange(
    n,
    hidden_ref, cot_ref, weight_ref, mask_ref,
    gathered, cot_feat, mask_out, out_ref,
    weight, total, other_part, mask,
    weight_sem, hid_send, hid_recv, cot_send, cot_recv, pair_send, pair_recv, own_sem,
):
    rows, cols = hidden_ref.shape
    feats = weight_ref.shape[0]
    f_tiles = feats // BLOCK
    chunk = cols // CHUNKS
    tiles = chunk // BLOCK
    half_feats = feats // 2
    tokens = n * rows
    me = lax.axis_index("row")
    core = lax.axis_index("col")
    half = n // 2
    mesh_id = pl.DeviceIdType.MESH

    spot = jnp.where(lax.rem(me, 2) == 0, me // 2, n - 1 - me // 2)

    def row_of(place):
        place = lax.rem(place + n, n)
        return jnp.where(place < half, 2 * place, 2 * (n - 1 - place) + 1)

    places = [
        [row_of(spot - back) for back in range(half + 1)],
        [row_of(spot + back) for back in range(half + 1)],
    ]
    heads = [places[1][1], places[0][1]]

    barrier = pltpu.get_barrier_semaphore()
    for d in range(1, n):
        pl.semaphore_signal(
            barrier, inc=1, device_id={"row": lax.rem(me + d, n)}, device_id_type=mesh_id
        )
    pl.semaphore_signal(barrier, inc=1, device_id={"col": 1 - core}, device_id_type=mesh_id)

    def span(c):
        return pl.ds(c * chunk, chunk)

    my_half = pl.ds(pl.multiple_of(core * half_feats, 128), half_feats)

    def cot_piece(to):
        return cot_ref.at[:, pl.ds(pl.multiple_of(to * feats + core * half_feats, 128), half_feats)]

    pl.semaphore_wait(barrier, n)

    def hop(way, h, c, back):
        here = gathered.at[places[way][back], :, span(c)]
        return pltpu.make_async_remote_copy(
            src_ref=hidden_ref.at[:, span(c)] if back == 0 else here,
            dst_ref=here,
            send_sem=hid_send.at[way],
            recv_sem=hid_recv.at[way, h - 1, c],
            device_id={"row": heads[way]},
            device_id_type=mesh_id,
        )

    for c in range(CHUNKS):
        for way in range(2):
            hop(way, 1, c, 0).start()

    cot_copies = []
    for d in range(1, n):
        to = lax.rem(me + d, n)
        copy = pltpu.make_async_remote_copy(
            src_ref=cot_piece(to),
            dst_ref=cot_feat.at[me, :, my_half],
            send_sem=cot_send.at[d - 1],
            recv_sem=cot_recv.at[d - 1],
            device_id={"row": to},
            device_id_type=mesh_id,
        )
        copy.start()
        cot_copies.append(copy)
    locals_ = [
        pltpu.make_async_copy(hidden_ref, gathered.at[me], own_sem.at[0]),
        pltpu.make_async_copy(cot_piece(me), cot_feat.at[me, :, my_half], own_sem.at[1]),
        pltpu.make_async_copy(mask_ref, mask, own_sem.at[2]),
        pltpu.make_async_copy(mask_ref, mask_out, own_sem.at[3]),
    ]
    for copy in locals_:
        copy.start()
    loads = []
    for c in range(CHUNKS):
        load = pltpu.make_async_copy(
            weight_ref.at[:, span(c)], weight.at[:, span(c)], weight_sem.at[c]
        )
        load.start()
        loads.append(load)
    total[...] = jnp.zeros_like(total)

    def last_way(c):
        return 0 if c < CHUNKS // 2 else 1

    for h in range(1, half):
        for c in range(CHUNKS):
            for way in range(2):
                hop(way, h, c, h).wait_recv()
                if h + 1 < half or last_way(c) == way:
                    hop(way, h + 1, c, h).start()
    for copy in locals_:
        copy.wait()
    for copy in cot_copies:
        copy.wait_recv()
    mine = cot_feat.at[:, :, my_half]
    cot_pair = pltpu.make_async_remote_copy(
        src_ref=mine, dst_ref=mine,
        send_sem=pair_send.at[0], recv_sem=pair_recv.at[0],
        device_id={"col": 1 - core}, device_id_type=mesh_id,
    )
    cot_pair.start()

    def multiply(c):
        loads[c].wait()
        block = gathered[:, :, c * chunk:(c + 1) * chunk].reshape(tokens, chunk)
        for f in range(f_tiles):
            parts = []
            for t in range(tiles):
                factor = mask[me * f_tiles + f, core * (CHUNKS * tiles) + c * tiles + t]
                factor = factor.astype(jnp.float32).astype(jnp.bfloat16)
                parts.append(block[:, t * BLOCK:(t + 1) * BLOCK] * factor)
            picked = jnp.concatenate(parts, axis=1)
            lanes = slice(f * BLOCK, (f + 1) * BLOCK)
            total[:, lanes] += lax.dot_general(
                picked,
                weight[lanes, c * chunk:(c + 1) * chunk],
                (((1,), (1,)), ((), ())),
                preferred_element_type=jnp.float32,
            )

    for i in range(CHUNKS // 2):
        for c in (i, i + CHUNKS // 2):
            hop(last_way(c), half, c, half).wait_recv()
            multiply(c)

    kept_rows = tokens // 2
    pair = pltpu.make_async_remote_copy(
        src_ref=total.at[pl.ds(pl.multiple_of((1 - core) * kept_rows, 8), kept_rows)],
        dst_ref=other_part,
        send_sem=pair_send.at[1], recv_sem=pair_recv.at[1],
        device_id={"col": 1 - core}, device_id_type=mesh_id,
    )
    pair.start()
    for way in range(2):
        all_sent = gathered.at[pl.ds(0, n - 1), :, pl.ds(0, cols // 2)]
        pltpu.make_async_remote_copy(
            src_ref=all_sent, dst_ref=all_sent,
            send_sem=hid_send.at[way], recv_sem=hid_recv.at[way, 0, 0],
            device_id={"row": heads[way]}, device_id_type=mesh_id,
        ).wait_send()
    for copy in cot_copies:
        copy.wait_send()
    cot_pair.wait()
    pair.wait()
    mine = total[pl.ds(pl.multiple_of(core * kept_rows, 8), kept_rows), :]
    out_ref[...] = (mine + other_part[...]).astype(out_ref.dtype)


def outer(gathered, cot_feat, mask_ref, grad_ref):
    n, rows, cols = gathered.shape
    tokens = n * rows
    feats = cot_feat.shape[2]
    f_tiles = feats // BLOCK
    height = grad_ref.shape[0]
    tiles = cols // BLOCK
    me = lax.axis_index("row")
    core = lax.axis_index("col")
    step = pl.program_id(0)
    f = step // (BLOCK // height)
    left = cot_feat[:, :, pl.ds(pl.multiple_of(step * height, height), height)]
    left = left.reshape(tokens, height)
    for t in range(tiles):
        factor = mask_ref[me * f_tiles + f, core * tiles + t]
        factor = factor.astype(jnp.float32).astype(jnp.bfloat16)
        lanes = slice(t * BLOCK, (t + 1) * BLOCK)
        grad_ref[:, lanes] = lax.dot_general(
            left,
            gathered[:, :, lanes].reshape(tokens, BLOCK) * factor,
            (((0,), (0,)), ((), ())),
            preferred_element_type=jnp.float32,
        )


def grad_of(gathered, cot_feat, block_mask):
    n, rows, cols = gathered.shape
    feats = cot_feat.shape[2]
    vmem = pl.BlockSpec(memory_space=pltpu.VMEM)
    return pl.pallas_call(
        outer,
        grid=(feats // HEIGHT,),
        out_shape=jax.ShapeDtypeStruct((feats, cols), jnp.float32),
        in_specs=[vmem, vmem, pl.BlockSpec(memory_space=pltpu.SMEM)],
        out_specs=pl.BlockSpec((HEIGHT, cols), lambda step: (step, 0)),
        compiler_params=pltpu.CompilerParams(vmem_limit_bytes=40 * 1024 * 1024),
        cost_estimate=pl.CostEstimate(
            flops=2 * n * rows * feats * cols,
            bytes_accessed=4 * feats * cols,
            transcendentals=0,
        ),
    )(gathered, cot_feat, block_mask)


def tiled(n, hidden, cotangent, weight_t, block_mask):
    rows, cols = hidden.shape
    feats = weight_t.shape[0]
    tokens = n * rows
    half = n // 2
    vmem = pl.BlockSpec(memory_space=pltpu.VMEM)
    hbm = pl.BlockSpec(memory_space=pltpu.HBM)
    gathered, cot_feat, mask, output = pl.pallas_call(
        functools.partial(exchange, n),
        out_shape=(
            jax.ShapeDtypeStruct((n, rows, cols), jnp.bfloat16),
            jax.ShapeDtypeStruct((n, rows, feats), jnp.bfloat16),
            jax.ShapeDtypeStruct(block_mask.shape, jnp.int32),
            jax.ShapeDtypeStruct((tokens // 2, feats), jnp.bfloat16),
        ),
        in_specs=[hbm, hbm, hbm, hbm],
        out_specs=(vmem, vmem, vmem, vmem),
        scratch_shapes=[
            pltpu.VMEM((feats, cols), jnp.bfloat16),
            pltpu.VMEM((tokens, feats), jnp.float32),
            pltpu.VMEM((tokens // 2, feats), jnp.float32),
            pltpu.SMEM(block_mask.shape, jnp.int32),
            pltpu.SemaphoreType.DMA((CHUNKS,)),
            pltpu.SemaphoreType.DMA((2,)),
            pltpu.SemaphoreType.DMA((2, half, CHUNKS)),
            pltpu.SemaphoreType.DMA((n - 1,)),
            pltpu.SemaphoreType.DMA((n - 1,)),
            pltpu.SemaphoreType.DMA((2,)),
            pltpu.SemaphoreType.DMA((2,)),
            pltpu.SemaphoreType.DMA((4,)),
        ],
        compiler_params=pltpu.CompilerParams(
            collective_id=0, has_side_effects=True, vmem_limit_bytes=40 * 1024 * 1024
        ),
        cost_estimate=pl.CostEstimate(
            flops=2 * tokens * feats * cols,
            bytes_accessed=2 * feats * cols,
            transcendentals=0,
        ),
    )(
        *(
            pltpu.with_memory_space_constraint(array, pltpu.HBM)
            for array in (hidden, cotangent, weight_t, block_mask)
        )
    )
    return output, grad_of(gathered, cot_feat, mask)


def solution(mesh):
    n = mesh.shape["row"]

    def local(hidden, cotangent, weight_t, block_mask):
        feats, cols = weight_t.shape
        whole_tiles = feats % BLOCK == 0 and cols % (CHUNKS * BLOCK) == 0
        if whole_tiles and n % 2 == 0 and mesh.shape["col"] == 2:
            return tiled(n, hidden, cotangent, weight_t, block_mask)
        return general(hidden, cotangent, weight_t, block_mask)

    return jax.shard_map(
        local,
        mesh=mesh,
        in_specs=(P(("groups", "row"), "col"), P(("groups", "row"), None), P("row", "col"), P()),
        out_specs=(P(("groups", "col"), "row"), P(("groups", "row"), "col")),
        check_vma=False,
    )
```
